512 devices in a mesh: ctx: 64 (over z_lo, y, core), head: 8 (over x, z_hi).
Axes of the slice: x: 4, y: 4, z: 16 (z_hi: 2, z_lo: 8; z = z_hi * 8 + z_lo), core: 2. Of those that a mesh axis runs over, the one named last changes fastest.
Arguments:
- block_order: int32 [64], P('ctx'), may hold values from 0 to 63, as said below
- query_b: bfloat16 [16384, 32, 128], P('ctx', 'head'), may hold values from -6 to 6
- key_b: bfloat16 [16384, 8, 128], P('ctx', 'head'), may hold values from -6 to 6
- value_b: bfloat16 [16384, 8, 128], P('ctx', 'head'), may hold values from -6 to 6
- out_weight: bfloat16 [32, 128, 4096], P('head', None, 'ctx'), may hold values from -0.1875 to 0.1875
- query_a: bfloat16 [16384, 32, 128], P('ctx', 'head'), may hold values from -6 to 6
- key_a: bfloat16 [16384, 8, 128], P('ctx', 'head'), may hold values from -6 to 6
- value_a: bfloat16 [16384, 8, 128], P('ctx', 'head'), may hold values from -6 to 6
- grad_a: bfloat16 [16384, 32, 128], P('ctx', 'head'), may hold values from -6 to 6
Outputs:
- out_b: bfloat16 [16384, 4096], P('ctx', 'head')
- grad_query_a: bfloat16 [16384, 32, 128], P('ctx', 'head')
- grad_key_a: bfloat16 [16384, 8, 128], P('ctx', 'head')
- grad_value_a: bfloat16 [16384, 8, 128], P('ctx', 'head')
The draws below stay inside these ranges and needn't reach their ends.
Inputs may be any that keep to these rules, and one draw needn't show every extreme that they name: block_order[p] = (p - c) mod (64) for one offset c: cycle neighbours hold neighbouring sequence blocks, and the sequence begins at cycle position c.
All inputs are finite; a program needn't handle non-finite values.
Results may differ from the reference program's by a relative error of at most 0.019.
Values may be sent and summed in bfloat16 or wider, within the bound.
A program may use at most 64 MiB of HBM per device.

```python
import jax
import jax.numpy as jnp
from jax import lax

D = 4096
HEADS = 32
KV_HEADS = 8
HEAD_DIM = 128
ROWS = 256
HOPS = 4
WINDOW = 1024
TOKENS = 16384


def draw_block_order(key, part):
    key = jax.random.fold_in(key, 5)
    blocks = TOKENS // ROWS
    offset = jax.random.randint(key, (), 0, blocks)
    return ((jnp.arange(blocks, dtype=jnp.int32) - offset) % blocks).astype(jnp.int32)


def draw_query_b(key, part):
    own_key = jax.random.fold_in(key, 11)
    base = jax.random.truncated_normal(own_key, -4.0, 4.0, (TOKENS, HEADS, HEAD_DIM), jnp.float32)
    return base.astype(jnp.bfloat16)


def draw_key_b(key, part):
    own_key = jax.random.fold_in(key, 12)
    base = jax.random.truncated_normal(own_key, -4.0, 4.0, (TOKENS, KV_HEADS, HEAD_DIM), jnp.float32)
    return base.astype(jnp.bfloat16)


def draw_query_a(key, part):
    own_key = jax.random.fold_in(key, 13)
    base = jax.random.truncated_normal(own_key, -4.0, 4.0, (TOKENS, HEADS, HEAD_DIM), jnp.float32)
    return base.astype(jnp.bfloat16)


def draw_key_a(key, part):
    own_key = jax.random.fold_in(key, 14)
    base = jax.random.truncated_normal(own_key, -4.0, 4.0, (TOKENS, KV_HEADS, HEAD_DIM), jnp.float32)
    return base.astype(jnp.bfloat16)


def with_spikes(drawn, rng, source, target, parts, factor):
    owner, partner = [(jnp.arange(drawn.shape[axis_at]) // (drawn.shape[axis_at] // parts)).reshape([-1 if axis == axis_at else 1 for axis in range(drawn.ndim)]) for axis_at in (source, target)]
    chosen = jax.random.permutation(rng, parts)[partner]
    strong = (owner == chosen) | (owner == (partner + parts // 2) % parts)
    return jnp.where(strong, factor * drawn, drawn)


def block_levels(key, dims, pieces, least, high):
    def one(position, parts):
        draws = jax.random.uniform(jax.random.fold_in(jax.random.fold_in(key, 6), position), (parts,), jnp.float32, least / len(pieces), high / len(pieces))
        return jnp.repeat(jnp.exp(draws), dims[position] // parts).reshape((-1,) + (1,) * (len(dims) - position - 1))

    factor_of = one(*pieces[0])
    for cut in pieces[1:]:
        factor_of = factor_of * one(*cut)
    return factor_of


def centred(key, dims, scale, reach, pieces=(), kind=jnp.bfloat16):
    values = scale * jax.random.normal(key, dims, jnp.float32)
    if pieces:
        values = values * block_levels(key, dims, pieces, -0.22, 0.18)
    return jnp.clip(values, -reach, reach).astype(kind)


def gaussian_with(rng, dims, scale, bound, cuts, heavy, held_as=jnp.bfloat16):
    result = scale * jax.random.normal(rng, dims, jnp.float32)
    if cuts:
        result = result * block_levels(rng, dims, cuts, -0.22, 0.18)
    return jnp.clip(with_spikes(result, jax.random.fold_in(rng, 3), *heavy), -bound, bound).astype(held_as)


def setup_inputs(seed: int = 0) -> dict:
    keys = jax.random.split(jax.random.key(seed), 10)
    block_order = draw_block_order(jax.random.fold_in(keys[9], 71), 0)
    query_b = draw_query_b(jax.random.fold_in(keys[9], 71), 0)
    key_b = draw_key_b(jax.random.fold_in(keys[9], 71), 0)
    value_b = centred(keys[3], (TOKENS, KV_HEADS, HEAD_DIM), 1.0, 6.0, ((0, 64), (1, 8)))
    out_weight = gaussian_with(keys[4], (HEADS, HEAD_DIM, D), (HEADS * HEAD_DIM) ** -0.5, 0.1875, ((0, 8), (2, 64)), (0, 2, 32, 2.75))
    query_a = draw_query_a(jax.random.fold_in(keys[9], 71), 0)
    key_a = draw_key_a(jax.random.fold_in(keys[9], 71), 0)
    value_a = centred(keys[7], (TOKENS, KV_HEADS, HEAD_DIM), 1.0, 6.0, ((0, 64), (1, 8)))
    grad_a = centred(keys[8], (TOKENS, HEADS, HEAD_DIM), 1.0, 6.0, ((0, 64), (1, 8)))
    return dict(block_order=block_order, query_b=query_b, key_b=key_b, value_b=value_b, out_weight=out_weight, query_a=query_a, key_a=key_a, value_a=value_a, grad_a=grad_a)


def visible_pairs(block_index):
    query_pos = block_index * ROWS + jnp.arange(ROWS, dtype=jnp.int32)
    key_pos = block_index * ROWS - HOPS * ROWS + jnp.arange((HOPS + 1) * ROWS, dtype=jnp.int32)
    distance = query_pos[:, None] - key_pos[None, :]
    return (distance >= 0) & (distance < WINDOW) & (key_pos[None, :] >= 0)


def masked_scores(query_rows, key_rows, allowed):
    query4 = query_rows.astype(jnp.float32).reshape(ROWS, KV_HEADS, HEADS // KV_HEADS, HEAD_DIM)
    scores = jnp.einsum("rkgd,ckd->kgrc", query4, key_rows.astype(jnp.float32)) * (HEAD_DIM ** -0.5)
    return jnp.where(allowed, scores, -jnp.inf), query4


def softmax_pass(scores, value_rows):
    top = jnp.max(scores, axis=-1)
    powers = jnp.exp(scores - top[..., None])
    totals = jnp.sum(powers, axis=-1)
    weights = lax.optimization_barrier(powers.astype(jnp.bfloat16)).astype(jnp.float32)
    mixed = jnp.einsum("kgrc,ckd->kgrd", weights, value_rows.astype(jnp.float32)) / totals[..., None]
    return mixed, top, totals


def reference(block_order, query_b, key_b, value_b, out_weight, query_a, key_a, value_a, grad_a):
    blocks = TOKENS // ROWS
    span = (HOPS + 1) * ROWS
    score_scale = HEAD_DIM ** -0.5
    inverse = jnp.zeros((blocks,), jnp.int32).at[block_order].set(jnp.arange(blocks, dtype=jnp.int32))

    def reorder(array, order):
        shaped = array.reshape((blocks, ROWS) + array.shape[1:])
        return shaped[order].reshape(array.shape)

    def padded(array):
        front = jnp.zeros((HOPS * ROWS,) + array.shape[1:], array.dtype)
        return jnp.concatenate([front, reorder(array, inverse)], axis=0)

    seq_query_b = reorder(query_b, inverse)
    pad_key_b = padded(key_b)
    pad_value_b = padded(value_b)

    def forward_block(block_index):
        offset = (block_index * ROWS).astype(jnp.int32)
        query_rows = lax.dynamic_slice_in_dim(seq_query_b, offset, ROWS, 0)
        key_rows = lax.dynamic_slice_in_dim(pad_key_b, offset, span, 0)
        value_rows = lax.dynamic_slice_in_dim(pad_value_b, offset, span, 0)
        scores, query4 = masked_scores(query_rows, key_rows, visible_pairs(block_index))
        mixed, top, totals = softmax_pass(scores, value_rows)
        return jnp.transpose(mixed, (2, 0, 1, 3)).reshape(ROWS, HEADS * HEAD_DIM).astype(jnp.bfloat16)

    attended = lax.map(forward_block, jnp.arange(blocks, dtype=jnp.int32)).reshape(TOKENS, HEADS * HEAD_DIM)
    projected = jnp.dot(attended, out_weight.reshape(HEADS * HEAD_DIM, D), preferred_element_type=jnp.float32)
    out_b = reorder(projected.astype(jnp.bfloat16), block_order)

    seq_query_a = reorder(query_a, inverse)
    seq_grad_a = reorder(grad_a, inverse)
    pad_key_a = padded(key_a)
    pad_value_a = padded(value_a)

    def backward_block(carry, block_index):
        grad_keys, grad_values = carry
        offset = (block_index * ROWS).astype(jnp.int32)
        query_rows = lax.dynamic_slice_in_dim(seq_query_a, offset, ROWS, 0)
        grad_rows = lax.dynamic_slice_in_dim(seq_grad_a, offset, ROWS, 0)
        key_rows = lax.dynamic_slice_in_dim(pad_key_a, offset, span, 0)
        value_rows = lax.dynamic_slice_in_dim(pad_value_a, offset, span, 0)
        scores, query4 = masked_scores(query_rows, key_rows, visible_pairs(block_index))
        outputs, top, totals = softmax_pass(scores, value_rows)
        log_totals = top + jnp.log(totals)
        grad4 = grad_rows.astype(jnp.float32).reshape(ROWS, KV_HEADS, HEADS // KV_HEADS, HEAD_DIM)
        deltas = jnp.sum(jnp.transpose(grad4, (1, 2, 0, 3)) * outputs, axis=-1)
        probs = jnp.exp(scores - log_totals[..., None])
        probs_low = lax.optimization_barrier(probs.astype(jnp.bfloat16)).astype(jnp.float32)
        value_terms = jnp.einsum("kgrc,rkgd->ckd", probs_low, grad4)
        grad_probs = jnp.einsum("rkgd,ckd->kgrc", grad4, value_rows.astype(jnp.float32))
        grad_scores = probs * (grad_probs - deltas[..., None])
        grad_scores = lax.optimization_barrier(grad_scores.astype(jnp.bfloat16)).astype(jnp.float32)
        query_terms = jnp.einsum("kgrc,ckd->rkgd", grad_scores, key_rows.astype(jnp.float32)) * score_scale
        key_terms = jnp.einsum("kgrc,rkgd->ckd", grad_scores, query4) * score_scale
        grad_keys = lax.dynamic_update_slice_in_dim(
            grad_keys, lax.dynamic_slice_in_dim(grad_keys, offset, span, 0) + key_terms, offset, 0)
        grad_values = lax.dynamic_update_slice_in_dim(
            grad_values, lax.dynamic_slice_in_dim(grad_values, offset, span, 0) + value_terms, offset, 0)
        return (grad_keys, grad_values), query_terms.reshape(ROWS, HEADS, HEAD_DIM).astype(jnp.bfloat16)

    zeros_pad = jnp.zeros(((blocks + HOPS) * ROWS, KV_HEADS, HEAD_DIM), jnp.float32)
    (grad_keys, grad_values), grad_queries = lax.scan(
        backward_block, (zeros_pad, zeros_pad), jnp.arange(blocks, dtype=jnp.int32))
    grad_query_a = reorder(grad_queries.reshape(TOKENS, HEADS, HEAD_DIM), block_order)
    grad_key_a = reorder(grad_keys[HOPS * ROWS:].astype(jnp.bfloat16), block_order)
    grad_value_a = reorder(grad_values[HOPS * ROWS:].astype(jnp.bfloat16), block_order)
    return (out_b, grad_query_a, grad_key_a, grad_value_a)
```

```python
import functools
import math

import jax
import jax.numpy as jnp
from jax import lax
from jax.experimental import pallas as pl
from jax.experimental.pallas import tpu as pltpu
from jax.sharding import PartitionSpec as P

Z, Y, X = 8, 4, 4
ROWS, HEADS, DIM = 256, 4, 128
QROWS = ROWS * HEADS
HOPS = 4
CHUNKS, CHUNK = 4, 256
SCALE = DIM**-0.5
SCALE2 = SCALE * math.log2(math.e)
NEG = -1e30
MESH = pl.DeviceIdType.MESH
F32, BF16 = jnp.float32, jnp.bfloat16


def dot(a, b, dims):
    return lax.dot_general(a, b, (dims, ((), ())), preferred_element_type=F32)


def nt(a, b):
    return dot(a, b, ((1,), (1,)))


def nn(a, b):
    return dot(a, b, ((1,), (0,)))


class Place:
    def __init__(self, ctx, head):
        self.ctx, self.head = ctx, head
        self.z, self.y, self.core = ctx // 8, (ctx // 2) % 4, ctx % 2
        self.x, self.half = head // 2, head % 2

    def at(self, z=None, y=None, core=None, x=None, half=None):
        z = self.z if z is None else z
        y = self.y if y is None else y
        core = self.core if core is None else core
        x = self.x if x is None else x
        half = self.half if half is None else half
        return ((z * Y + y) * 2 + core, x * 2 + half)

    def sibling(self):
        return self.at(core=1 - self.core)

    def along_x(self, by):
        return self.at(x=(self.x + by + X) % X)

    def along_y(self, by):
        return self.at(y=(self.y + by + Y) % Y)

    def quad(self, by):
        return self.at(z=self.z // 4 * 4 + (self.z + by + 4) % 4)

    def other_half(self):
        return self.at(half=1 - self.half)

    def chip(self, by):
        return ((self.ctx + 2 * by + 64) % 64, self.head)

    def turned(self, by):
        return ((self.head + by) % Z * 8 + self.ctx % 8, self.z)

    def turned_from(self, by):
        return (self.head * 8 + self.ctx % 8, (self.z - by + Z) % Z)


def kernel(
    order_ref, qb_ref, kb_ref, vb_ref, w_ref, qa_ref, ka_ref, va_ref, ga_ref,
    out_ref, dq_ref, dk_ref, dv_ref,
    kv_b, kv_a, wt, att, s_buf, dp_buf, rows_buf, acc, dqt, m_buf, l_buf, d_buf,
    dkv, gsend, grecv, send_sem, recv_sem,
):
    me = Place(lax.axis_index("ctx"), lax.axis_index("head"))
    core = me.core
    own_block = order_ref[0]

    sources = [me.sibling(), me.other_half()]
    sources += [me.along_x(by) for by in (1, 2, 3)]
    sources += [me.along_y(by) for by in (1, 2, 3)]
    sources += [me.quad(by) for by in (1, 2, 3)]
    sources += [me.chip(by) for by in (1, 2, -1, -2)]
    sources += [me.turned_from(1), me.turned_from(5)]
    barrier = pltpu.get_barrier_semaphore()
    for source in sources:
        pl.semaphore_signal(barrier, inc=1, device_id=source, device_id_type=MESH)

    started = []

    def send(src, dst, target):
        at = len(started)
        copy = pltpu.make_async_remote_copy(
            src_ref=src, dst_ref=dst, send_sem=send_sem.at[at], recv_sem=recv_sem.at[at],
            device_id=target, device_id_type=MESH,
        )
        copy.start()
        started.append(copy)
        return copy

    kv_b[0, 0] = kb_ref[...]
    kv_b[0, 1] = vb_ref[...]
    kv_a[0, 0] = ka_ref[...]
    kv_a[0, 1] = va_ref[...]

    def masked(s, hop, c):
        if hop not in (0, HOPS):
            return s
        key = lax.broadcasted_iota(jnp.int32, s.shape, 0)
        token = c * (CHUNK // HEADS) + lax.broadcasted_iota(jnp.int32, s.shape, 1) // HEADS
        return jnp.where(token >= key if hop == 0 else token < key, s, NEG)

    def stats(s, hop, c):
        top = jnp.max(s, axis=0, keepdims=True)
        if hop == 0:
            return top, top * SCALE2, None
        seen = own_block >= hop
        before = m_buf[c]
        top = jnp.maximum(before, jnp.where(seen, top, NEG))
        return top, jnp.where(seen, top * SCALE2, -NEG), jnp.exp2((before - top) * SCALE2)

    def forward_b(hop):
        vt = kv_b[hop, 1].T

        def step(c, _):
            s = masked(nt(kv_b[hop, 0], qb_ref[pl.ds(c * CHUNK, CHUNK), :]), hop, c)
            top, minus, factor = stats(s, hop, c)
            p = jnp.exp2(s * SCALE2 - minus)
            total = jnp.sum(p, axis=0, keepdims=True)
            part = nn(vt, p.astype(BF16))
            m_buf[c] = top
            if hop == 0:
                l_buf[c] = total
                acc[c] = part
            else:
                l_buf[c] = l_buf[c] * factor + total
                acc[c] = acc[c] * factor + part
            return 0

        lax.fori_loop(0, CHUNKS, step, 0)

    def forward_a(hop):
        def step(c, _):
            s = masked(nt(kv_a[hop, 0], qa_ref[pl.ds(c * CHUNK, CHUNK), :]), hop, c)
            s_buf[hop, c] = s
            top, minus, factor = stats(s, hop, c)
            p = jnp.exp2(s * SCALE2 - minus)
            total = jnp.sum(p, axis=0, keepdims=True)
            dp = nt(kv_a[hop, 1], ga_ref[pl.ds(c * CHUNK, CHUNK), :])
            dp_buf[hop, c] = dp
            part = jnp.sum(p * dp, axis=0, keepdims=True)
            m_buf[c] = top
            if hop == 0:
                l_buf[c] = total
                d_buf[c] = part
            else:
                l_buf[c] = l_buf[c] * factor + total
                d_buf[c] = d_buf[c] * factor + part
            return 0

        lax.fori_loop(0, CHUNKS, step, 0)

    def backward_a(hop):
        kt = kv_a[hop, 0].T
        dkv[...] = jnp.zeros_like(dkv)

        def step(c, _):
            part = pl.ds(c * CHUNK, CHUNK)
            log_total = l_buf[c]
            if hop:
                log_total = jnp.where(own_block >= hop, log_total, -NEG)
            probs = jnp.exp2(s_buf[hop, c] * SCALE2 - log_total)
            low = probs.astype(BF16)
            ds = (probs * (dp_buf[hop, c] - d_buf[c])).astype(BF16)
            dkv[0] += nn(ds, qa_ref[part, :])
            dkv[1] += nn(low, ga_ref[part, :])
            if hop == 1:
                dqt[c] = nn(kt, ds)
            else:
                dqt[c] += nn(kt, ds)
            return 0

        lax.fori_loop(0, CHUNKS, step, 0)

    forward_b(0)
    pl.semaphore_wait(barrier, len(sources))

    def halo_first(kv):
        return [send(kv.at[0], kv.at[2 * by], me.chip(by)) for by in (1, 2)]

    halo_b = halo_first(kv_b)
    turn = [
        send(w_ref, wt.at[core, me.y, (me.head + 1) % 4, (me.head + 1) % Z // 4], me.turned(by))
        for by in (1, 5)
    ]
    halo_a = halo_first(kv_a)

    def halo_rest(kv, halo):
        halo[0].wait_recv()
        first = send(kv.at[2 * core], kv.at[1], me.sibling())
        halo[1].wait_recv()
        second = send(kv.at[2 + 2 * core], kv.at[3], me.sibling())
        return first, second

    rest_b = halo_rest(kv_b, halo_b)
    forward_b(2)
    forward_b(4)
    rest_b[0].wait_recv()
    forward_b(1)
    rest_b[1].wait_recv()
    forward_b(3)

    def finish_b(c, _):
        rows_buf[pl.ds(c * CHUNK, CHUNK), :] = (acc[c] / l_buf[c]).T
        return 0

    lax.fori_loop(0, CHUNKS, finish_b, 0)
    across, beside = [], []
    for h in range(HEADS):
        att[me.head, h] = rows_buf[pl.ds(h, ROWS, stride=HEADS), :].astype(BF16)
        mine = att.at[me.head, h]
        across.append(send(mine, mine, me.other_half()))
        for by in (1, 2, 3):
            beside.append(send(mine, mine, me.along_x(by)))

    own = me.z % 4
    in_quad, in_row, in_chip = [], [], []
    for copy in turn:
        copy.wait_recv()
    pair = wt.at[core, me.y, own]
    for by in (1, 2, 3):
        in_quad.append(send(pair, pair, me.quad(by)))

    def spread(q):
        pair = wt.at[core, me.y, q]
        got = [send(pair, pair, me.along_y(by)) for by in (1, 3, 2)]
        in_chip.append(send(pair, pair, me.sibling()))
        return [(copy, by, q) for copy, by in zip(got, (1, 3, 2))]

    in_row += spread(own)

    rest_a = halo_rest(kv_a, halo_a)
    forward_a(0)
    forward_a(2)
    for by in (1, 2, 3):
        in_quad[by - 1].wait_recv()
        in_row += spread((me.z + 4 - by) % 4)
        if by == 1:
            forward_a(4)
        elif by == 2:
            rest_a[0].wait_recv()
            forward_a(1)
    rest_a[1].wait_recv()
    forward_a(3)

    def finish_stats(c, _):
        d_buf[c] = d_buf[c] / l_buf[c]
        l_buf[c] = m_buf[c] * SCALE2 + jnp.log2(l_buf[c])
        return 0

    lax.fori_loop(0, CHUNKS, finish_stats, 0)

    def to_sibling(copy, by, q):
        copy.wait_recv()
        pair = wt.at[core, (me.y - by + Y) % Y, q]
        in_chip.append(send(pair, pair, me.sibling()))

    passed = []

    def to_row(h):
        across[h].wait_recv()
        theirs = att.at[me.head + 1 - 2 * me.half, h]
        for by in (1, 2, 3):
            passed.append(send(theirs, theirs, me.along_x(by)))

    def to_send(at):
        gsend[at, 0] = (dkv[0] * SCALE).astype(BF16)
        gsend[at, 1] = dkv[1].astype(BF16)

    def add(at, weight):
        dkv[0] += grecv[at, 0].astype(F32) * (weight / SCALE)
        dkv[1] += grecv[at, 1].astype(F32) * weight

    backward_a(1)
    to_send(0)
    grad_1 = send(gsend.at[0], grecv.at[0], me.sibling())
    for item in in_row[:3]:
        to_sibling(*item)
    backward_a(3)
    to_send(1)
    grad_3 = send(gsend.at[1], grecv.at[1], me.sibling())
    for item in in_row[3:6]:
        to_sibling(*item)
    backward_a(2)
    grad_1.wait_recv()
    grad_3.wait_recv()
    add(1 - core, 1.0)
    to_send(2)
    grad_2 = send(gsend.at[2], grecv.at[2], me.chip(-1))
    backward_a(4)
    add(1, core.astype(F32))
    to_send(3)
    grad_4 = send(gsend.at[3], grecv.at[3], me.chip(-2))
    to_row(0)
    for item in in_row[6:9]:
        to_sibling(*item)
    backward_a(0)
    to_row(1)
    for item in in_row[9:]:
        to_sibling(*item)

    def finish_dq(c, _):
        dq_ref[pl.ds(c * CHUNK, CHUNK), :] = (dqt[c] * SCALE).T.astype(BF16)
        return 0

    lax.fori_loop(0, CHUNKS, finish_dq, 0)
    add(0, (1 - core).astype(F32))
    to_row(2)
    to_row(3)
    grad_2.wait_recv()
    grad_4.wait_recv()
    add(2, 1.0)
    add(3, 1.0)
    dk_ref[...] = (dkv[0] * SCALE).astype(BF16)
    dv_ref[...] = dkv[1].astype(BF16)

    for copy in beside + in_chip + passed:
        copy.wait_recv()
    total = None
    for q in range(4):
        for hi in range(2):
            head = (hi * 4 + q - 1) % Z
            rhs = jnp.concatenate(
                [
                    jnp.concatenate([wt[k, y, q, hi, h] for y in range(Y) for k in range(2)], axis=0)
                    for h in range(HEADS)
                ],
                axis=1,
            )
            lhs = jnp.concatenate([att[head, h] for h in range(HEADS)], axis=1)
            term = nt(lhs, rhs)
            total = term if total is None else total + term
    out_ref[...] = total.astype(BF16)
    for copy in started:
        copy.wait_send()


SENDS = 100


def local(block_order, query_b, key_b, value_b, out_weight, query_a, key_a, value_a, grad_a):
    flat_q = lambda a: a.reshape(QROWS, DIM)
    flat_k = lambda a: a.reshape(ROWS, DIM)
    vmem = pl.BlockSpec(memory_space=pltpu.VMEM)
    out, dq, dk, dv = pl.pallas_call(
        kernel,
        out_shape=(
            jax.ShapeDtypeStruct((ROWS, 512), BF16),
            jax.ShapeDtypeStruct((QROWS, DIM), BF16),
            jax.ShapeDtypeStruct((ROWS, DIM), BF16),
            jax.ShapeDtypeStruct((ROWS, DIM), BF16),
        ),
        in_specs=[pl.BlockSpec(memory_space=pltpu.SMEM)] + [vmem] * 8,
        out_specs=(vmem,) * 4,
        scratch_shapes=[
            pltpu.VMEM((5, 2, ROWS, DIM), BF16),
            pltpu.VMEM((5, 2, ROWS, DIM), BF16),
            pltpu.VMEM((2, Y, 4, 2, HEADS, 64, DIM), BF16),
            pltpu.VMEM((8, HEADS, ROWS, DIM), BF16),
            pltpu.VMEM((5, CHUNKS, ROWS, CHUNK), F32),
            pltpu.VMEM((5, CHUNKS, ROWS, CHUNK), F32),
            pltpu.VMEM((QROWS, DIM), F32),
            pltpu.VMEM((CHUNKS, DIM, CHUNK), F32),
            pltpu.VMEM((CHUNKS, DIM, CHUNK), F32),
            pltpu.VMEM((CHUNKS, 1, CHUNK), F32),
            pltpu.VMEM((CHUNKS, 1, CHUNK), F32),
            pltpu.VMEM((CHUNKS, 1, CHUNK), F32),
            pltpu.VMEM((2, ROWS, DIM), F32),
            pltpu.VMEM((4, 2, ROWS, DIM), BF16),
            pltpu.VMEM((4, 2, ROWS, DIM), BF16),
            pltpu.SemaphoreType.DMA((SENDS,)),
            pltpu.SemaphoreType.DMA((SENDS,)),
        ],
        compiler_params=pltpu.CompilerParams(
            collective_id=0, has_side_effects=True, vmem_limit_bytes=48 * 2**20
        ),
        name="attention",
    )(
        block_order, flat_q(query_b), flat_k(key_b), flat_k(value_b),
        jnp.transpose(out_weight, (0, 2, 1)),
        flat_q(query_a), flat_k(key_a), flat_k(value_a), flat_q(grad_a),
    )
    flat = (ROWS, 1, DIM)
    return out, dq.reshape(ROWS, HEADS, DIM), dk.reshape(flat), dv.reshape(flat)


def solution(mesh):
    heads = P("ctx", "head", None)
    return jax.shard_map(
        local,
        mesh=mesh,
        in_specs=(P("ctx"), heads, heads, heads, P("head", None, "ctx"), heads, heads, heads, heads),
        out_specs=(P("ctx", "head"), heads, heads, heads),
        check_vma=False,
    )
```

```python
import functools
import math

import jax
import jax.numpy as jnp
from jax import lax
from jax.experimental import pallas as pl
from jax.experimental.pallas import tpu as pltpu
from jax.sharding import PartitionSpec as P

Z, Y, X = 8, 4, 4
ROWS, HEADS, DIM = 256, 4, 128
QROWS = ROWS * HEADS
HOPS = 4
CHUNKS, CHUNK = 4, 256
SCALE = DIM**-0.5
SCALE2 = SCALE * math.log2(math.e)
NEG = -1e30
MESH = pl.DeviceIdType.MESH
F32, BF16 = jnp.float32, jnp.bfloat16


def dot(a, b, dims):
    return lax.dot_general(a, b, (dims, ((), ())), preferred_element_type=F32)


def nt(a, b):
    return dot(a, b, ((1,), (1,)))


def nn(a, b):
    return dot(a, b, ((1,), (0,)))


class Place:
    def __init__(self, ctx, head):
        self.ctx, self.head = ctx, head
        self.z, self.y, self.core = ctx // 8, (ctx // 2) % 4, ctx % 2
        self.x, self.half = head // 2, head % 2

    def at(self, z=None, y=None, core=None, x=None, half=None):
        z = self.z if z is None else z
        y = self.y if y is None else y
        core = self.core if core is None else core
        x = self.x if x is None else x
        half = self.half if half is None else half
        return ((z * Y + y) * 2 + core, x * 2 + half)

    def sibling(self):
        return self.at(core=1 - self.core)

    def along_x(self, by):
        return self.at(x=(self.x + by + X) % X)

    def along_y(self, by):
        return self.at(y=(self.y + by + Y) % Y)

    def quad(self, by):
        return self.at(z=self.z // 4 * 4 + (self.z + by + 4) % 4)

    def other_half(self):
        return self.at(half=1 - self.half)

    def chip(self, by):
        return ((self.ctx + 2 * by + 64) % 64, self.head)

    def turned(self, by):
        return ((self.head + by) % Z * 8 + self.ctx % 8, self.z)

    def turned_from(self, by):
        return (self.head * 8 + self.ctx % 8, (self.z - by + Z) % Z)


def kernel(
    order_ref, qb_hbm, kb_hbm, vb_hbm, w_ref, qa_hbm, ka_hbm, va_hbm, ga_hbm,
    out_ref, dq_ref, dk_ref, dv_ref,
    qb_ref, qa_ref, ga_ref,
    kv_b, kv_a, wt, att, s_buf, dp_buf, rows_buf, acc, dqt, m_buf, l_buf, d_buf, mb_buf, lb_buf, vt_buf, sa_buf,
    dkv, gsend, grecv, send_sem, recv_sem, load_sem,
):
    me = Place(lax.axis_index("ctx"), lax.axis_index("head"))
    core = me.core
    own_block = order_ref[0]

    sources = [me.other_half(), me.turned_from(1), me.turned_from(5)]
    sources += [me.chip(by) for by in (1, 2, -1, -2)]
    sources += [me.along_x(by) for by in (1, 2, 3)]
    sources += [me.along_y(by) for by in (1, 2, 3)]
    sources += [me.quad(by) for by in (1, 2, 3)]
    sources += [me.sibling()]
    barrier = pltpu.get_barrier_semaphore()
    for source in sources:
        pl.semaphore_signal(barrier, inc=1, device_id=source, device_id_type=MESH)

    loads = [
        (kb_hbm, kv_b.at[0, 0]), (qb_hbm, qb_ref), (vb_hbm, kv_b.at[0, 1]),
        (ka_hbm, kv_a.at[0, 0]), (qa_hbm, qa_ref), (va_hbm, kv_a.at[0, 1]), (ga_hbm, ga_ref),
    ]
    loads = [
        pltpu.make_async_copy(src, dst, load_sem.at[at]) for at, (src, dst) in enumerate(loads)
    ]
    for load in loads:
        load.start()

    started = []

    def send(src, dst, target):
        at = len(started)
        copy = pltpu.make_async_remote_copy(
            src_ref=src, dst_ref=dst, send_sem=send_sem.at[at], recv_sem=recv_sem.at[at],
            device_id=target, device_id_type=MESH,
        )
        copy.start()
        started.append(copy)
        return copy

    def masked(s, hop, c):
        if hop not in (0, HOPS):
            return s
        key = lax.broadcasted_iota(jnp.int32, s.shape, 0)
        token = c * (CHUNK // HEADS) + lax.broadcasted_iota(jnp.int32, s.shape, 1) // HEADS
        return jnp.where(token >= key if hop == 0 else token < key, s, NEG)

    def stats(s, hop, c):
        top = jnp.max(s, axis=0, keepdims=True)
        if hop == 0:
            return top, top * SCALE2, None
        seen = own_block >= hop
        before = m_buf[c]
        top = jnp.maximum(before, jnp.where(seen, top, NEG))
        return top, jnp.where(seen, top * SCALE2, -NEG), jnp.exp2((before - top) * SCALE2)

    def scores(kv, q_ref, hop, c):
        return masked(nt(kv[hop, 0], q_ref[pl.ds(c * CHUNK, CHUNK), :]), hop, c)

    def own_b():
        vt = kv_b[0, 1].T

        def step(c, _):
            s = scores(kv_b, qb_ref, 0, c)
            top = jnp.max(s, axis=0, keepdims=True)
            p = jnp.exp2((s - top) * SCALE2)
            mb_buf[c] = top
            lb_buf[c] = jnp.sum(p, axis=0, keepdims=True)
            acc[c] = nn(vt, p.astype(BF16))
            return 0

        lax.fori_loop(0, CHUNKS, step, 0)

    def scores_b(hop):
        def step(c, _):
            s_buf[hop, c] = scores(kv_b, qb_ref, hop, c)
            return 0

        lax.fori_loop(0, CHUNKS, step, 0)

    def rest_of_b(c):
        before = mb_buf[c]
        top = before
        for hop in (1, 2, 3, 4):
            if hop in (1, 3):
                s_buf[hop, c] = scores(kv_b, qb_ref, hop, c)
            block_top = jnp.max(s_buf[hop, c], axis=0, keepdims=True)
            top = jnp.maximum(top, jnp.where(own_block >= hop, block_top, NEG))
        factor = jnp.exp2((before - top) * SCALE2)
        total = lb_buf[c] * factor
        weighted = acc[c] * factor
        for hop in (1, 2, 3, 4):
            minus = jnp.where(own_block >= hop, top * SCALE2, -NEG)
            p = jnp.exp2(s_buf[hop, c] * SCALE2 - minus)
            total += jnp.sum(p, axis=0, keepdims=True)
            weighted += nn(vt_buf[hop], p.astype(BF16))
        rows_buf[...] = (weighted / total).T
        for h in range(HEADS):
            att[me.head, c, h] = rows_buf[pl.ds(h, CHUNK // HEADS, stride=HEADS), :].astype(BF16)

    def forward_a(hop):
        def step(c, _):
            s = scores(kv_a, qa_ref, hop, c)
            sa_buf[hop, c] = s
            top, minus, factor = stats(s, hop, c)
            p = jnp.exp2(s * SCALE2 - minus)
            total = jnp.sum(p, axis=0, keepdims=True)
            dp = nt(kv_a[hop, 1], ga_ref[pl.ds(c * CHUNK, CHUNK), :])
            dp_buf[hop, c] = dp
            part = jnp.sum(p * dp, axis=0, keepdims=True)
            m_buf[c] = top
            if hop == 0:
                l_buf[c] = total
                d_buf[c] = part
            else:
                l_buf[c] = l_buf[c] * factor + total
                d_buf[c] = d_buf[c] * factor + part
            return 0

        lax.fori_loop(0, CHUNKS, step, 0)

    def backward_a(hop):
        kt = kv_a[hop, 0].T
        dkv[...] = jnp.zeros_like(dkv)

        def step(c, _):
            part = pl.ds(c * CHUNK, CHUNK)
            log_total = l_buf[c]
            if hop:
                log_total = jnp.where(own_block >= hop, log_total, -NEG)
            probs = jnp.exp2(sa_buf[hop, c] * SCALE2 - log_total)
            low = probs.astype(BF16)
            ds = (probs * (dp_buf[hop, c] - d_buf[c])).astype(BF16)
            dkv[0] += nn(ds, qa_ref[part, :])
            dkv[1] += nn(low, ga_ref[part, :])
            if hop == 1:
                dqt[c] = nn(kt, ds)
            else:
                dqt[c] += nn(kt, ds)
            return 0

        lax.fori_loop(0, CHUNKS, step, 0)

    for load in loads[:3]:
        load.wait()
    own_b()
    for load in loads[3:]:
        load.wait()
    forward_a(0)
    pl.semaphore_wait(barrier, len(sources))

    def halo_first(kv):
        return [send(kv.at[0], kv.at[2 * by], me.chip(by)) for by in (1, 2)]

    halo_b = halo_first(kv_b)
    turn = [
        send(w_ref, wt.at[core, me.y, (me.head + 1) % 4, (me.head + 1) % Z // 4], me.turned(by))
        for by in (1, 5)
    ]
    halo_a = halo_first(kv_a)

    halo_b[0].wait_recv()
    rest_b = [send(kv_b.at[2 * core], kv_b.at[1], me.sibling())]
    vt_buf[2] = kv_b[2, 1].T
    scores_b(2)
    halo_b[1].wait_recv()
    rest_b.append(send(kv_b.at[2 + 2 * core], kv_b.at[3], me.sibling()))
    vt_buf[4] = kv_b[4, 1].T
    scores_b(4)
    for copy, hop in zip(rest_b, (1, 3)):
        copy.wait_recv()
        vt_buf[hop] = kv_b[hop, 1].T

    own = me.z % 4
    in_quad, in_row, in_chip = [], [], []

    def spread(q):
        pair = wt.at[core, me.y, q]
        got = [send(pair, pair, me.along_y(by)) for by in (1, 3, 2)]
        in_chip.append(send(pair, pair, me.sibling()))
        in_row.append([(copy, by, q) for copy, by in zip(got, (1, 3, 2))])

    def weight_turned():
        for copy in turn:
            copy.wait_recv()
        pair = wt.at[core, me.y, own]
        for by in (1, 3, 2):
            in_quad.append(send(pair, pair, me.quad(by)))
        spread(own)

    def weight_quad(by):
        in_quad[(1, 3, 2).index(by)].wait_recv()
        spread((me.z + 4 - by) % 4)

    def weight_row(at):
        for copy, by, q in in_row[at]:
            copy.wait_recv()
            pair = wt.at[core, (me.y - by + Y) % Y, q]
            in_chip.append(send(pair, pair, me.sibling()))

    across, beside, passed = [], [], []
    for c in range(CHUNKS):
        rest_of_b(c)
        if c == 0:
            weight_turned()
        mine = att.at[me.head, c]
        across.append(send(mine, mine, me.other_half()))
        for by in (1, 3, 2):
            beside.append(send(mine, mine, me.along_x(by)))

    def to_row(c):
        across[c].wait_recv()
        theirs = att.at[me.head + 1 - 2 * me.half, c]
        for by in (1, 3, 2):
            passed.append(send(theirs, theirs, me.along_x(by)))

    halo_a[0].wait_recv()
    rest_a = [send(kv_a.at[2 * core], kv_a.at[1], me.sibling())]
    forward_a(2)
    halo_a[1].wait_recv()
    rest_a.append(send(kv_a.at[2 + 2 * core], kv_a.at[3], me.sibling()))
    forward_a(4)
    rest_a[0].wait_recv()
    forward_a(1)
    rest_a[1].wait_recv()
    forward_a(3)

    def finish_stats(c, _):
        d_buf[c] = d_buf[c] / l_buf[c]
        l_buf[c] = m_buf[c] * SCALE2 + jnp.log2(l_buf[c])
        return 0

    lax.fori_loop(0, CHUNKS, finish_stats, 0)

    def to_send(at):
        gsend[at, 0] = (dkv[0] * SCALE).astype(BF16)
        gsend[at, 1] = dkv[1].astype(BF16)

    def add(at, weight):
        dkv[0] += grecv[at, 0].astype(F32) * (weight / SCALE)
        dkv[1] += grecv[at, 1].astype(F32) * weight

    weight_row(0)
    backward_a(1)
    to_send(0)
    grad_1 = send(gsend.at[0], grecv.at[0], me.sibling())
    weight_quad(1)
    backward_a(3)
    to_send(1)
    grad_3 = send(gsend.at[1], grecv.at[1], me.sibling())
    weight_quad(3)
    to_row(0)
    backward_a(2)
    grad_1.wait_recv()
    grad_3.wait_recv()
    add(1 - core, 1.0)
    to_send(2)
    grad_2 = send(gsend.at[2], grecv.at[2], me.chip(-1))
    weight_quad(2)
    to_row(1)
    backward_a(4)
    add(1, core.astype(F32))
    to_send(3)
    grad_4 = send(gsend.at[3], grecv.at[3], me.chip(-2))
    weight_row(1)
    backward_a(0)

    def finish_dq(c, _):
        dq_ref[pl.ds(c * CHUNK, CHUNK), :] = (dqt[c] * SCALE).T.astype(BF16)
        return 0

    lax.fori_loop(0, CHUNKS, finish_dq, 0)
    add(0, (1 - core).astype(F32))
    to_row(2)
    weight_row(2)
    to_row(3)
    weight_row(3)
    grad_2.wait_recv()
    grad_4.wait_recv()
    add(2, 1.0)
    add(3, 1.0)
    dk_ref[...] = (dkv[0] * SCALE).astype(BF16)
    dv_ref[...] = dkv[1].astype(BF16)

    for copy in beside + in_chip + passed:
        copy.wait_recv()
    total = None
    for q in range(4):
        for hi in range(2):
            head = (hi * 4 + q - 1) % Z
            rhs = jnp.concatenate(
                [
                    jnp.concatenate([wt[k, y, q, hi, h] for y in range(Y) for k in range(2)], axis=0)
                    for h in range(HEADS)
                ],
                axis=1,
            )
            lhs = jnp.concatenate(
                [
                    jnp.concatenate([att[head, c, h] for c in range(CHUNKS)], axis=0)
                    for h in range(HEADS)
                ],
                axis=1,
            )
            term = nt(lhs, rhs)
            total = term if total is None else total + term
    out_ref[...] = total.astype(BF16)
    for copy in started:
        copy.wait_send()
    assert len(started) == SENDS


SENDS = 73


def local(block_order, query_b, key_b, value_b, out_weight, query_a, key_a, value_a, grad_a):
    flat_q = lambda a: a.reshape(QROWS, DIM)
    flat_k = lambda a: a.reshape(ROWS, DIM)
    vmem = pl.BlockSpec(memory_space=pltpu.VMEM)
    out, dq, dk, dv = pl.pallas_call(
        kernel,
        out_shape=(
            jax.ShapeDtypeStruct((ROWS, 512), BF16),
            jax.ShapeDtypeStruct((QROWS, DIM), BF16),
            jax.ShapeDtypeStruct((ROWS, DIM), BF16),
            jax.ShapeDtypeStruct((ROWS, DIM), BF16),
        ),
        in_specs=[pl.BlockSpec(memory_space=pltpu.SMEM)] + [pl.BlockSpec(memory_space=pl.ANY)] * 8,
        out_specs=(vmem,) * 4,
        scratch_shapes=[
            pltpu.VMEM((QROWS, DIM), BF16),
            pltpu.VMEM((QROWS, DIM), BF16),
            pltpu.VMEM((QROWS, DIM), BF16),
            pltpu.VMEM((5, 2, ROWS, DIM), BF16),
            pltpu.VMEM((5, 2, ROWS, DIM), BF16),
            pltpu.VMEM((2, Y, 4, 2, HEADS, 64, DIM), BF16),
            pltpu.VMEM((8, CHUNKS, HEADS, CHUNK // HEADS, DIM), BF16),
            pltpu.VMEM((5, CHUNKS, ROWS, CHUNK), F32),
            pltpu.VMEM((5, CHUNKS, ROWS, CHUNK), F32),
            pltpu.VMEM((CHUNK, DIM), F32),
            pltpu.VMEM((CHUNKS, DIM, CHUNK), F32),
            pltpu.VMEM((CHUNKS, DIM, CHUNK), F32),
            pltpu.VMEM((CHUNKS, 1, CHUNK), F32),
            pltpu.VMEM((CHUNKS, 1, CHUNK), F32),
            pltpu.VMEM((CHUNKS, 1, CHUNK), F32),
            pltpu.VMEM((CHUNKS, 1, CHUNK), F32),
            pltpu.VMEM((CHUNKS, 1, CHUNK), F32),
            pltpu.VMEM((5, DIM, ROWS), BF16),
            pltpu.VMEM((5, CHUNKS, ROWS, CHUNK), F32),
            pltpu.VMEM((2, ROWS, DIM), F32),
            pltpu.VMEM((4, 2, ROWS, DIM), BF16),
            pltpu.VMEM((4, 2, ROWS, DIM), BF16),
            pltpu.SemaphoreType.DMA((SENDS,)),
            pltpu.SemaphoreType.DMA((SENDS,)),
            pltpu.SemaphoreType.DMA((7,)),
        ],
        compiler_params=pltpu.CompilerParams(
            collective_id=0, has_side_effects=True, vmem_limit_bytes=62 * 2**20
        ),
        name="attention",
    )(
        block_order, flat_q(query_b), flat_k(key_b), flat_k(value_b),
        jnp.transpose(out_weight, (0, 2, 1)),
        flat_q(query_a), flat_k(key_a), flat_k(value_a), flat_q(grad_a),
    )
    flat = (ROWS, 1, DIM)
    return out, dq.reshape(ROWS, HEADS, DIM), dk.reshape(flat), dv.reshape(flat)


def solution(mesh):
    heads = P("ctx", "head", None)
    return jax.shard_map(
        local,
        mesh=mesh,
        in_specs=(P("ctx"), heads, heads, heads, P("head", None, "ctx"), heads, heads, heads, heads),
        out_specs=(P("ctx", "head"), heads, heads, heads),
        check_vma=False,
    )
```

```python
import functools
import math

import jax
import jax.numpy as jnp
from jax import lax
from jax.experimental import pallas as pl
from jax.experimental.pallas import tpu as pltpu
from jax.sharding import PartitionSpec as P

Z, Y, X = 8, 4, 4
ROWS, HEADS, DIM = 256, 4, 128
QROWS = ROWS * HEADS
HOPS = 4
CHUNKS, CHUNK = 4, 256
SCALE = DIM**-0.5
SCALE2 = SCALE * math.log2(math.e)
NEG = -1e30
MESH = pl.DeviceIdType.MESH
F32, BF16 = jnp.float32, jnp.bfloat16


def dot(a, b, dims):
    return lax.dot_general(a, b, (dims, ((), ())), preferred_element_type=F32)


def nt(a, b):
    return dot(a, b, ((1,), (1,)))


def nn(a, b):
    return dot(a, b, ((1,), (0,)))


class Place:
    def __init__(self, ctx, head):
        self.ctx, self.head = ctx, head
        self.z, self.y, self.core = ctx // 8, (ctx // 2) % 4, ctx % 2
        self.x, self.half = head // 2, head % 2

    def at(self, z=None, y=None, core=None, x=None, half=None):
        z = self.z if z is None else z
        y = self.y if y is None else y
        core = self.core if core is None else core
        x = self.x if x is None else x
        half = self.half if half is None else half
        return ((z * Y + y) * 2 + core, x * 2 + half)

    def sibling(self):
        return self.at(core=1 - self.core)

    def along_x(self, by):
        return self.at(x=(self.x + by + X) % X)

    def along_y(self, by):
        return self.at(y=(self.y + by + Y) % Y)

    def quad(self, by):
        return self.at(z=self.z // 4 * 4 + (self.z + by + 4) % 4)

    def other_half(self):
        return self.at(half=1 - self.half)

    def chip(self, by):
        return ((self.ctx + 2 * by + 64) % 64, self.head)

    def turned(self, by):
        return ((self.head + by) % Z * 8 + self.ctx % 8, self.z)

    def turned_from(self, by):
        return (self.head * 8 + self.ctx % 8, (self.z - by + Z) % Z)


def kernel(
    order_ref, qb_hbm, kb_hbm, vb_hbm, w_ref, qa_hbm, ka_hbm, va_hbm, ga_hbm,
    out_ref, dq_ref, dk_ref, dv_ref,
    qb_ref, qa_ref, ga_ref,
    kv_b, kv_a, wt, att, s_buf, dp_buf, rows_buf, acc, dqt, m_buf, l_buf, d_buf, mb_buf, lb_buf, vt_buf, sa_buf,
    dkv, gsend, grecv, send_sem, recv_sem, shared_sem, load_sem, even_sem, far_sem,
):
    me = Place(lax.axis_index("ctx"), lax.axis_index("head"))
    core = me.core
    own_block = order_ref[0]

    sources = [me.other_half(), me.turned_from(1), me.turned_from(5)]
    sources += [me.chip(by) for by in (1, 2, -1, -2)]
    sources += [me.along_x(by) for by in (1, 2, 3)]
    sources += [me.along_y(by) for by in (1, 2, 3)]
    sources += [me.quad(by) for by in (1, 2, 3)]
    sources += [me.sibling()]
    barrier = pltpu.get_barrier_semaphore()
    for source in sources:
        pl.semaphore_signal(barrier, inc=1, device_id=source, device_id_type=MESH)

    loads = [
        (kb_hbm, kv_b.at[0, 0]), (qb_hbm, qb_ref), (vb_hbm, kv_b.at[0, 1]),
        (ka_hbm, kv_a.at[0, 0]), (qa_hbm, qa_ref), (va_hbm, kv_a.at[0, 1]), (ga_hbm, ga_ref),
    ]
    loads = [
        pltpu.make_async_copy(src, dst, load_sem.at[at]) for at, (src, dst) in enumerate(loads)
    ]
    for load in loads:
        load.start()

    started = []

    taken = [0, 0]

    def own_sem(sems, side):
        taken[side] += 1
        return sems.at[taken[side] - 1]

    def send(src, dst, target, send_on=None, recv_on=None):
        copy = pltpu.make_async_remote_copy(
            src_ref=src, dst_ref=dst,
            send_sem=own_sem(send_sem, 0) if send_on is None else shared_sem.at[send_on],
            recv_sem=own_sem(recv_sem, 1) if recv_on is None else shared_sem.at[recv_on],
            device_id=target, device_id_type=MESH,
        )
        copy.start()
        if send_on is None:
            started.append(copy)
        return copy

    def all_of(ref, send_on, recv_on):
        return pltpu.make_async_remote_copy(
            src_ref=ref, dst_ref=ref, send_sem=shared_sem.at[send_on],
            recv_sem=shared_sem.at[recv_on], device_id=me.sibling(), device_id_type=MESH,
        )

    def masked(s, hop, c):
        if hop not in (0, HOPS):
            return s
        key = lax.broadcasted_iota(jnp.int32, s.shape, 0)
        token = c * (CHUNK // HEADS) + lax.broadcasted_iota(jnp.int32, s.shape, 1) // HEADS
        return jnp.where(token >= key if hop == 0 else token < key, s, NEG)

    def stats(s, hop, c):
        top = jnp.max(s, axis=0, keepdims=True)
        if hop == 0:
            return top, top * SCALE2, None
        seen = own_block >= hop
        before = m_buf[c]
        top = jnp.maximum(before, jnp.where(seen, top, NEG))
        return top, jnp.where(seen, top * SCALE2, -NEG), jnp.exp2((before - top) * SCALE2)

    def scores(kv, q_ref, hop, c):
        return masked(nt(kv[hop, 0], q_ref[pl.ds(c * CHUNK, CHUNK), :]), hop, c)

    def own_b():
        vt = kv_b[0, 1].T

        def step(c, _):
            s = scores(kv_b, qb_ref, 0, c)
            top = jnp.max(s, axis=0, keepdims=True)
            p = jnp.exp2((s - top) * SCALE2)
            mb_buf[c] = top
            lb_buf[c] = jnp.sum(p, axis=0, keepdims=True)
            acc[c] = nn(vt, p.astype(BF16))
            return 0

        lax.fori_loop(0, CHUNKS, step, 0)

    def scores_b(hop):
        def step(c, _):
            s_buf[hop, c] = scores(kv_b, qb_ref, hop, c)
            return 0

        lax.fori_loop(0, CHUNKS, step, 0)

    def rest_of_b(c):
        before = mb_buf[c]
        top = before
        for hop in (1, 2, 3, 4):
            if hop in (1, 3):
                s_buf[hop, c] = scores(kv_b, qb_ref, hop, c)
            block_top = jnp.max(s_buf[hop, c], axis=0, keepdims=True)
            top = jnp.maximum(top, jnp.where(own_block >= hop, block_top, NEG))
        factor = jnp.exp2((before - top) * SCALE2)
        total = lb_buf[c] * factor
        weighted = acc[c] * factor
        for hop in (1, 2, 3, 4):
            minus = jnp.where(own_block >= hop, top * SCALE2, -NEG)
            p = jnp.exp2(s_buf[hop, c] * SCALE2 - minus)
            total += jnp.sum(p, axis=0, keepdims=True)
            weighted += nn(vt_buf[hop], p.astype(BF16))
        rows_buf[...] = (weighted / total).T
        for h in range(HEADS):
            att[me.head, c, h] = rows_buf[pl.ds(h, CHUNK // HEADS, stride=HEADS), :].astype(BF16)

    def forward_a(hop):
        def step(c, _):
            s = scores(kv_a, qa_ref, hop, c)
            sa_buf[hop, c] = s
            top, minus, factor = stats(s, hop, c)
            p = jnp.exp2(s * SCALE2 - minus)
            total = jnp.sum(p, axis=0, keepdims=True)
            dp = nt(kv_a[hop, 1], ga_ref[pl.ds(c * CHUNK, CHUNK), :])
            dp_buf[hop, c] = dp
            part = jnp.sum(p * dp, axis=0, keepdims=True)
            m_buf[c] = top
            if hop == 0:
                l_buf[c] = total
                d_buf[c] = part
            else:
                l_buf[c] = l_buf[c] * factor + total
                d_buf[c] = d_buf[c] * factor + part
            return 0

        lax.fori_loop(0, CHUNKS, step, 0)

    def backward_a(hop):
        kt = kv_a[hop, 0].T
        dkv[...] = jnp.zeros_like(dkv)

        def step(c, _):
            part = pl.ds(c * CHUNK, CHUNK)
            log_total = l_buf[c]
            if hop:
                log_total = jnp.where(own_block >= hop, log_total, -NEG)
            probs = jnp.exp2(sa_buf[hop, c] * SCALE2 - log_total)
            low = probs.astype(BF16)
            ds = (probs * (dp_buf[hop, c] - d_buf[c])).astype(BF16)
            dkv[0] += nn(ds, qa_ref[part, :])
            dkv[1] += nn(low, ga_ref[part, :])
            if hop == 1:
                dqt[c] = nn(kt, ds)
            else:
                dqt[c] += nn(kt, ds)
            return 0

        lax.fori_loop(0, CHUNKS, step, 0)

    for load in loads[:3]:
        load.wait()
    own_b()
    for load in loads[3:]:
        load.wait()
    forward_a(0)
    pl.semaphore_wait(barrier, len(sources))

    even_chip = me.y % 2 == 0
    from_even = []

    class EvenOnly:
        def __init__(self, src, dst, target, recv):
            self.copy = pltpu.make_async_remote_copy(
                src_ref=src, dst_ref=dst, send_sem=even_sem.at[len(from_even)], recv_sem=recv,
                device_id=target, device_id_type=MESH,
            )
            pl.when(even_chip)(self.copy.start)
            from_even.append(self.copy)

        def wait_recv(self):
            self.copy.wait_recv()

    def halo_direct(kv):
        return [send(kv.at[0], kv.at[2 * by], me.chip(by)) for by in (1, 2)]

    def halo_first(kv, at):
        first = send(kv.at[0], kv.at[2], me.chip(1))
        return [first, EvenOnly(kv.at[0], kv.at[4], me.chip(2), far_sem.at[at])]

    def hand_on(kv, at):
        return EvenOnly(kv.at[2], kv.at[4], me.chip(1), far_sem.at[at])

    halo_b = halo_direct(kv_b)
    turn = [
        send(w_ref, wt.at[core, me.y, (me.head + 1) % 4, (me.head + 1) % Z // 4], me.turned(by))
        for by in (1, 5)
    ]
    halo_a = halo_first(kv_a, 1)

    halo_b[0].wait_recv()
    rest_b = [send(kv_b.at[2 * core], kv_b.at[1], me.sibling())]
    vt_buf[2] = kv_b[2, 1].T
    scores_b(2)
    halo_b[1].wait_recv()
    rest_b.append(send(kv_b.at[2 + 2 * core], kv_b.at[3], me.sibling()))
    vt_buf[4] = kv_b[4, 1].T
    scores_b(4)
    for copy, hop in zip(rest_b, (1, 3)):
        copy.wait_recv()
        vt_buf[hop] = kv_b[hop, 1].T

    own = me.z % 4
    in_quad, in_row = [], []

    def spread(q):
        pair = wt.at[core, me.y, q]
        got = [send(pair, pair, me.along_y(by), send_on=2) for by in (1, 3, 2)]
        send(pair, pair, me.sibling(), send_on=1, recv_on=0)
        in_row.append([(copy, by, q) for copy, by in zip(got, (1, 3, 2))])

    def weight_turned():
        for copy in turn:
            copy.wait_recv()
        pair = wt.at[core, me.y, own]
        for by in (1, 3, 2):
            in_quad.append(send(pair, pair, me.quad(by)))
        spread(own)

    def weight_quad(by):
        in_quad[(1, 3, 2).index(by)].wait_recv()
        spread((me.z + 4 - by) % 4)

    def weight_row(at):
        for copy, by, q in in_row[at]:
            copy.wait_recv()
            pair = wt.at[core, (me.y - by + Y) % Y, q]
            send(pair, pair, me.sibling(), send_on=1, recv_on=0)

    across = []
    for c in range(CHUNKS):
        rest_of_b(c)
        if c == 0:
            weight_turned()
        mine = att.at[me.head, c]
        across.append(send(mine, mine, me.other_half()))
        for by in (1, 3, 2):
            send(mine, mine, me.along_x(by), send_on=4, recv_on=3)

    def to_row(c):
        across[c].wait_recv()
        theirs = att.at[me.head + 1 - 2 * me.half, c]
        for by in (1, 3, 2):
            send(theirs, theirs, me.along_x(by), send_on=4, recv_on=3)

    halo_a[0].wait_recv()
    hand_on(kv_a, 1)
    rest_a = [send(kv_a.at[2 * core], kv_a.at[1], me.sibling())]
    forward_a(2)
    halo_a[1].wait_recv()
    rest_a.append(send(kv_a.at[2 + 2 * core], kv_a.at[3], me.sibling()))
    forward_a(4)
    rest_a[0].wait_recv()
    forward_a(1)
    rest_a[1].wait_recv()
    forward_a(3)

    def finish_stats(c, _):
        d_buf[c] = d_buf[c] / l_buf[c]
        l_buf[c] = m_buf[c] * SCALE2 + jnp.log2(l_buf[c])
        return 0

    lax.fori_loop(0, CHUNKS, finish_stats, 0)

    def to_send(at):
        gsend[at, 0] = (dkv[0] * SCALE).astype(BF16)
        gsend[at, 1] = dkv[1].astype(BF16)

    def add(at, weight):
        dkv[0] += grecv[at, 0].astype(F32) * (weight / SCALE)
        dkv[1] += grecv[at, 1].astype(F32) * weight

    weight_row(0)
    backward_a(1)
    to_send(0)
    grad_1 = send(gsend.at[0], grecv.at[0], me.sibling())
    weight_quad(1)
    backward_a(3)
    to_send(1)
    grad_3 = send(gsend.at[1], grecv.at[1], me.sibling())
    weight_quad(3)
    to_row(0)
    backward_a(2)
    grad_1.wait_recv()
    grad_3.wait_recv()
    add(1 - core, 1.0)
    to_send(2)
    grad_2 = send(gsend.at[2], grecv.at[2], me.chip(-1))
    weight_quad(2)
    to_row(1)
    backward_a(4)
    add(1, core.astype(F32))
    to_send(3)
    grad_4 = send(gsend.at[3], grecv.at[3], me.chip(-2))
    weight_row(1)
    backward_a(0)

    def finish_dq(c, _):
        dq_ref[pl.ds(c * CHUNK, CHUNK), :] = (dqt[c] * SCALE).T.astype(BF16)
        return 0

    lax.fori_loop(0, CHUNKS, finish_dq, 0)
    add(0, (1 - core).astype(F32))
    to_row(2)
    weight_row(2)
    to_row(3)
    weight_row(3)
    grad_2.wait_recv()
    grad_4.wait_recv()
    add(2, 1.0)
    add(3, 1.0)
    dk_ref[...] = (dkv[0] * SCALE).astype(BF16)
    dv_ref[...] = dkv[1].astype(BF16)

    in_chip = all_of(wt.at[1 - core], 1, 0)
    in_head = all_of(att.at[pl.ds(0, 6)], 4, 3)
    in_chip.wait_recv()
    in_head.wait_recv()
    total = None
    for q in range(4):
        for hi in range(2):
            head = (hi * 4 + q - 1) % Z
            rhs = jnp.concatenate(
                [
                    jnp.concatenate([wt[k, y, q, hi, h] for y in range(Y) for k in range(2)], axis=0)
                    for h in range(HEADS)
                ],
                axis=1,
            )
            lhs = jnp.concatenate(
                [
                    jnp.concatenate([att[head, c, h] for c in range(CHUNKS)], axis=0)
                    for h in range(HEADS)
                ],
                axis=1,
            )
            term = nt(lhs, rhs)
            total = term if total is None else total + term
    out_ref[...] = total.astype(BF16)
    for copy in started:
        copy.wait_send()
    in_chip.wait_send()
    in_head.wait_send()
    all_of(wt.at[0, pl.ds(0, 3)], 2, 0).wait_send()

    @pl.when(even_chip)
    def _():
        for copy in from_even:
            copy.wait_send()

    assert taken == [SENDS, RECVS], taken


SENDS, RECVS = 20, 32


def place(*refs):
    ins, outs, held, sems = refs[:4], refs[4:8], refs[8:12], refs[12]
    loads = [pltpu.make_async_copy(ins[i], held[i], sems.at[i]) for i in range(4)]
    for load in loads:
        load.start()
    stores = []
    for i in range(4):
        loads[i].wait()
        stores.append(pltpu.make_async_copy(held[i], outs[i], sems.at[4 + i]))
        stores[i].start()
    for store in stores:
        store.wait()


def local(block_order, query_b, key_b, value_b, out_weight, query_a, key_a, value_a, grad_a):
    flat_q = lambda a: a.reshape(QROWS, DIM)
    flat_k = lambda a: a.reshape(ROWS, DIM)
    vmem = pl.BlockSpec(memory_space=pltpu.VMEM)
    results = pl.pallas_call(
        kernel,
        out_shape=(
            jax.ShapeDtypeStruct((ROWS, 512), BF16),
            jax.ShapeDtypeStruct((QROWS, DIM), BF16),
            jax.ShapeDtypeStruct((ROWS, DIM), BF16),
            jax.ShapeDtypeStruct((ROWS, DIM), BF16),
        ),
        in_specs=[pl.BlockSpec(memory_space=pltpu.SMEM)] + [pl.BlockSpec(memory_space=pl.ANY)] * 8,
        out_specs=(vmem,) * 4,
        scratch_shapes=[
            pltpu.VMEM((QROWS, DIM), BF16),
            pltpu.VMEM((QROWS, DIM), BF16),
            pltpu.VMEM((QROWS, DIM), BF16),
            pltpu.VMEM((5, 2, ROWS, DIM), BF16),
            pltpu.VMEM((5, 2, ROWS, DIM), BF16),
            pltpu.VMEM((2, Y, 4, 2, HEADS, 64, DIM), BF16),
            pltpu.VMEM((8, CHUNKS, HEADS, CHUNK // HEADS, DIM), BF16),
            pltpu.VMEM((5, CHUNKS, ROWS, CHUNK), F32),
            pltpu.VMEM((5, CHUNKS, ROWS, CHUNK), F32),
            pltpu.VMEM((CHUNK, DIM), F32),
            pltpu.VMEM((CHUNKS, DIM, CHUNK), F32),
            pltpu.VMEM((CHUNKS, DIM, CHUNK), F32),
            pltpu.VMEM((CHUNKS, 1, CHUNK), F32),
            pltpu.VMEM((CHUNKS, 1, CHUNK), F32),
            pltpu.VMEM((CHUNKS, 1, CHUNK), F32),
            pltpu.VMEM((CHUNKS, 1, CHUNK), F32),
            pltpu.VMEM((CHUNKS, 1, CHUNK), F32),
            pltpu.VMEM((5, DIM, ROWS), BF16),
            pltpu.VMEM((5, CHUNKS, ROWS, CHUNK), F32),
            pltpu.VMEM((2, ROWS, DIM), F32),
            pltpu.VMEM((4, 2, ROWS, DIM), BF16),
            pltpu.VMEM((4, 2, ROWS, DIM), BF16),
            pltpu.SemaphoreType.DMA((SENDS,)),
            pltpu.SemaphoreType.DMA((RECVS,)),
            pltpu.SemaphoreType.DMA((5,)),
            pltpu.SemaphoreType.DMA((7,)),
            pltpu.SemaphoreType.DMA((2,)),
            pltpu.SemaphoreType.DMA((2,)),
        ],
        compiler_params=pltpu.CompilerParams(
            collective_id=0, has_side_effects=True, vmem_limit_bytes=62 * 2**20
        ),
        name="attention",
    )(
        block_order, flat_q(query_b), flat_k(key_b), flat_k(value_b),
        jnp.transpose(out_weight, (0, 2, 1)),
        flat_q(query_a), flat_k(key_a), flat_k(value_a), flat_q(grad_a),
    )
    shapes = tuple(jax.ShapeDtypeStruct(a.shape, a.dtype) for a in results)
    out, dq, dk, dv = pl.pallas_call(
        place,
        out_shape=shapes,
        in_specs=[pl.BlockSpec(memory_space=pl.ANY)] * 4,
        out_specs=(pl.BlockSpec(memory_space=pl.ANY),) * 4,
        scratch_shapes=[pltpu.VMEM(a.shape, a.dtype) for a in results]
        + [pltpu.SemaphoreType.DMA((8,))],
        compiler_params=pltpu.CompilerParams(vmem_limit_bytes=62 * 2**20),
        name="place",
    )(*results)
    flat = (ROWS, 1, DIM)
    return out, dq.reshape(ROWS, HEADS, DIM), dk.reshape(flat), dv.reshape(flat)


def solution(mesh):
    heads = P("ctx", "head", None)
    return jax.shard_map(
        local,
        mesh=mesh,
        in_specs=(P("ctx"), heads, heads, heads, P("head", None, "ctx"), heads, heads, heads, heads),
        out_specs=(P("ctx", "head"), heads, heads, heads),
        check_vma=False,
    )
```

```python
import functools
import math

import jax
import jax.numpy as jnp
from jax import lax
from jax.experimental import pallas as pl
from jax.experimental.pallas import tpu as pltpu
from jax.sharding import PartitionSpec as P

Z, Y, X = 8, 4, 4
ROWS, HEADS, DIM = 256, 4, 128
QROWS = ROWS * HEADS
HOPS = 4
CHUNKS, CHUNK = 4, 256
SCALE = DIM**-0.5
SCALE2 = SCALE * math.log2(math.e)
NEG = -1e30
MESH = pl.DeviceIdType.MESH
F32, BF16 = jnp.float32, jnp.bfloat16


def dot(a, b, dims):
    return lax.dot_general(a, b, (dims, ((), ())), preferred_element_type=F32)


def nt(a, b):
    return dot(a, b, ((1,), (1,)))


def nn(a, b):
    return dot(a, b, ((1,), (0,)))


class Place:
    def __init__(self, ctx, head):
        self.ctx, self.head = ctx, head
        self.z, self.y, self.core = ctx // 8, (ctx // 2) % 4, ctx % 2
        self.x, self.half = head // 2, head % 2

    def at(self, z=None, y=None, core=None, x=None, half=None):
        z = self.z if z is None else z
        y = self.y if y is None else y
        core = self.core if core is None else core
        x = self.x if x is None else x
        half = self.half if half is None else half
        return ((z * Y + y) * 2 + core, x * 2 + half)

    def sibling(self):
        return self.at(core=1 - self.core)

    def along_x(self, by):
        return self.at(x=(self.x + by + X) % X)

    def along_y(self, by):
        return self.at(y=(self.y + by + Y) % Y)

    def quad(self, by):
        return self.at(z=self.z // 4 * 4 + (self.z + by + 4) % 4)

    def other_half(self):
        return self.at(half=1 - self.half)

    def chip(self, by):
        return ((self.ctx + 2 * by + 64) % 64, self.head)

    def turned(self, by):
        return ((self.head + by) % Z * 8 + self.ctx % 8, self.z)

    def turned_from(self, by):
        return (self.head * 8 + self.ctx % 8, (self.z - by + Z) % Z)


def kernel(
    order_ref, qb_hbm, kb_hbm, vb_hbm, w_ref, qa_hbm, ka_hbm, va_hbm, ga_hbm,
    out_ref, dq_hbm, dk_hbm, dv_hbm,
    dq_ref, dk_ref, dv_ref,
    qb_ref, qa_ref, ga_ref,
    kv_b, kv_a, wt, att, s_buf, dp_buf, rows_buf, acc, dqt, m_buf, l_buf, d_buf, mb_buf, lb_buf, vt_buf, sa_buf,
    dkv, gsend, grecv, send_sem, recv_sem, shared_sem, load_sem, even_sem, far_sem,
):
    me = Place(lax.axis_index("ctx"), lax.axis_index("head"))
    core = me.core
    own_block = order_ref[0]

    sources = [me.other_half(), me.turned_from(1), me.turned_from(5)]
    sources += [me.chip(by) for by in (1, 2, -1, -2)]
    sources += [me.along_x(by) for by in (1, 2, 3)]
    sources += [me.along_y(by) for by in (1, 2, 3)]
    sources += [me.quad(by) for by in (1, 2, 3)]
    sources += [me.sibling()]
    barrier = pltpu.get_barrier_semaphore()
    for source in sources:
        pl.semaphore_signal(barrier, inc=1, device_id=source, device_id_type=MESH)

    loads = [
        (kb_hbm, kv_b.at[0, 0]), (qb_hbm, qb_ref), (vb_hbm, kv_b.at[0, 1]),
        (ka_hbm, kv_a.at[0, 0]), (qa_hbm, qa_ref), (va_hbm, kv_a.at[0, 1]), (ga_hbm, ga_ref),
    ]
    loads = [
        pltpu.make_async_copy(src, dst, load_sem.at[at]) for at, (src, dst) in enumerate(loads)
    ]
    for load in loads:
        load.start()

    started = []

    taken = [0, 0]

    def own_sem(sems, side):
        taken[side] += 1
        return sems.at[taken[side] - 1]

    def send(src, dst, target, send_on=None, recv_on=None):
        copy = pltpu.make_async_remote_copy(
            src_ref=src, dst_ref=dst,
            send_sem=own_sem(send_sem, 0) if send_on is None else shared_sem.at[send_on],
            recv_sem=own_sem(recv_sem, 1) if recv_on is None else shared_sem.at[recv_on],
            device_id=target, device_id_type=MESH,
        )
        copy.start()
        if send_on is None:
            started.append(copy)
        return copy

    def all_of(ref, send_on, recv_on):
        return pltpu.make_async_remote_copy(
            src_ref=ref, dst_ref=ref, send_sem=shared_sem.at[send_on],
            recv_sem=shared_sem.at[recv_on], device_id=me.sibling(), device_id_type=MESH,
        )

    def masked(s, hop, c):
        if hop not in (0, HOPS):
            return s
        key = lax.broadcasted_iota(jnp.int32, s.shape, 0)
        token = c * (CHUNK // HEADS) + lax.broadcasted_iota(jnp.int32, s.shape, 1) // HEADS
        return jnp.where(token >= key if hop == 0 else token < key, s, NEG)

    def stats(s, hop, c):
        top = jnp.max(s, axis=0, keepdims=True)
        if hop == 0:
            return top, top * SCALE2, None
        seen = own_block >= hop
        before = m_buf[c]
        top = jnp.maximum(before, jnp.where(seen, top, NEG))
        return top, jnp.where(seen, top * SCALE2, -NEG), jnp.exp2((before - top) * SCALE2)

    def scores(kv, q_ref, hop, c):
        return masked(nt(kv[hop, 0], q_ref[pl.ds(c * CHUNK, CHUNK), :]), hop, c)

    def own_b():
        vt = kv_b[0, 1].T

        def step(c, _):
            s = scores(kv_b, qb_ref, 0, c)
            top = jnp.max(s, axis=0, keepdims=True)
            p = jnp.exp2((s - top) * SCALE2)
            mb_buf[c] = top
            lb_buf[c] = jnp.sum(p, axis=0, keepdims=True)
            acc[c] = nn(vt, p.astype(BF16))
            return 0

        lax.fori_loop(0, CHUNKS, step, 0)

    def scores_b(hop):
        def step(c, _):
            s_buf[hop, c] = scores(kv_b, qb_ref, hop, c)
            return 0

        lax.fori_loop(0, CHUNKS, step, 0)

    def rest_of_b(c):
        before = mb_buf[c]
        top = before
        for hop in (1, 2, 3, 4):
            if hop in (1, 3):
                s_buf[hop, c] = scores(kv_b, qb_ref, hop, c)
            block_top = jnp.max(s_buf[hop, c], axis=0, keepdims=True)
            top = jnp.maximum(top, jnp.where(own_block >= hop, block_top, NEG))
        factor = jnp.exp2((before - top) * SCALE2)
        total = lb_buf[c] * factor
        weighted = acc[c] * factor
        for hop in (1, 2, 3, 4):
            minus = jnp.where(own_block >= hop, top * SCALE2, -NEG)
            p = jnp.exp2(s_buf[hop, c] * SCALE2 - minus)
            total += jnp.sum(p, axis=0, keepdims=True)
            weighted += nn(vt_buf[hop], p.astype(BF16))
        rows_buf[...] = (weighted / total).T
        for h in range(HEADS):
            att[me.head, c, h] = rows_buf[pl.ds(h, CHUNK // HEADS, stride=HEADS), :].astype(BF16)

    def forward_a(hop):
        def step(c, _):
            s = scores(kv_a, qa_ref, hop, c)
            sa_buf[hop, c] = s
            top, minus, factor = stats(s, hop, c)
            p = jnp.exp2(s * SCALE2 - minus)
            total = jnp.sum(p, axis=0, keepdims=True)
            dp = nt(kv_a[hop, 1], ga_ref[pl.ds(c * CHUNK, CHUNK), :])
            dp_buf[hop, c] = dp
            part = jnp.sum(p * dp, axis=0, keepdims=True)
            m_buf[c] = top
            if hop == 0:
                l_buf[c] = total
                d_buf[c] = part
            else:
                l_buf[c] = l_buf[c] * factor + total
                d_buf[c] = d_buf[c] * factor + part
            return 0

        lax.fori_loop(0, CHUNKS, step, 0)

    def backward_a(hop):
        kt = kv_a[hop, 0].T
        dkv[...] = jnp.zeros_like(dkv)

        def step(c, _):
            part = pl.ds(c * CHUNK, CHUNK)
            log_total = l_buf[c]
            if hop:
                log_total = jnp.where(own_block >= hop, log_total, -NEG)
            probs = jnp.exp2(sa_buf[hop, c] * SCALE2 - log_total)
            low = probs.astype(BF16)
            ds = (probs * (dp_buf[hop, c] - d_buf[c])).astype(BF16)
            dkv[0] += nn(ds, qa_ref[part, :])
            dkv[1] += nn(low, ga_ref[part, :])
            if hop == 1:
                dqt[c] = nn(kt, ds)
            else:
                dqt[c] += nn(kt, ds)
            return 0

        lax.fori_loop(0, CHUNKS, step, 0)

    for load in loads[:3]:
        load.wait()
    own_b()
    for load in loads[3:]:
        load.wait()
    forward_a(0)
    pl.semaphore_wait(barrier, len(sources))

    even_chip = me.y % 2 == 0
    from_even = []

    class EvenOnly:
        def __init__(self, src, dst, target, recv):
            self.copy = pltpu.make_async_remote_copy(
                src_ref=src, dst_ref=dst, send_sem=even_sem.at[len(from_even)], recv_sem=recv,
                device_id=target, device_id_type=MESH,
            )
            pl.when(even_chip)(self.copy.start)
            from_even.append(self.copy)

        def wait_recv(self):
            self.copy.wait_recv()

    def halo_direct(kv):
        return [send(kv.at[0], kv.at[2 * by], me.chip(by)) for by in (1, 2)]

    def halo_first(kv, at):
        first = send(kv.at[0], kv.at[2], me.chip(1))
        return [first, EvenOnly(kv.at[0], kv.at[4], me.chip(2), far_sem.at[at])]

    def hand_on(kv, at):
        return EvenOnly(kv.at[2], kv.at[4], me.chip(1), far_sem.at[at])

    halo_b = halo_direct(kv_b)
    turn = [
        send(w_ref, wt.at[core, me.y, (me.head + 1) % 4, (me.head + 1) % Z // 4], me.turned(by))
        for by in (1, 5)
    ]
    halo_a = halo_first(kv_a, 1)

    halo_b[0].wait_recv()
    rest_b = [send(kv_b.at[2 * core], kv_b.at[1], me.sibling())]
    vt_buf[2] = kv_b[2, 1].T
    scores_b(2)
    halo_b[1].wait_recv()
    rest_b.append(send(kv_b.at[2 + 2 * core], kv_b.at[3], me.sibling()))
    vt_buf[4] = kv_b[4, 1].T
    scores_b(4)
    for copy, hop in zip(rest_b, (1, 3)):
        copy.wait_recv()
        vt_buf[hop] = kv_b[hop, 1].T

    own = me.z % 4
    in_quad, in_row = [], []

    def spread(q):
        pair = wt.at[core, me.y, q]
        got = [send(pair, pair, me.along_y(by), send_on=2) for by in (1, 3, 2)]
        send(pair, pair, me.sibling(), send_on=1, recv_on=0)
        in_row.append([(copy, by, q) for copy, by in zip(got, (1, 3, 2))])

    def weight_turned():
        for copy in turn:
            copy.wait_recv()
        pair = wt.at[core, me.y, own]
        for by in (1, 3, 2):
            in_quad.append(send(pair, pair, me.quad(by)))
        spread(own)

    def weight_quad(by):
        in_quad[(1, 3, 2).index(by)].wait_recv()
        spread((me.z + 4 - by) % 4)

    def weight_row(at):
        for copy, by, q in in_row[at]:
            copy.wait_recv()
            pair = wt.at[core, (me.y - by + Y) % Y, q]
            send(pair, pair, me.sibling(), send_on=1, recv_on=0)

    across = []
    for c in range(CHUNKS):
        if c == 0:
            weight_turned()
        rest_of_b(c)
        mine = att.at[me.head, c]
        across.append(send(mine, mine, me.other_half()))
        for by in (1, 3, 2):
            send(mine, mine, me.along_x(by), send_on=4, recv_on=3)

    def to_row(c):
        across[c].wait_recv()
        theirs = att.at[me.head + 1 - 2 * me.half, c]
        for by in (1, 3, 2):
            send(theirs, theirs, me.along_x(by), send_on=4, recv_on=3)

    halo_a[0].wait_recv()
    hand_on(kv_a, 1)
    rest_a = [send(kv_a.at[2 * core], kv_a.at[1], me.sibling())]
    forward_a(2)
    halo_a[1].wait_recv()
    rest_a.append(send(kv_a.at[2 + 2 * core], kv_a.at[3], me.sibling()))
    forward_a(4)
    rest_a[0].wait_recv()
    forward_a(1)
    rest_a[1].wait_recv()
    forward_a(3)

    def finish_stats(c, _):
        d_buf[c] = d_buf[c] / l_buf[c]
        l_buf[c] = m_buf[c] * SCALE2 + jnp.log2(l_buf[c])
        return 0

    lax.fori_loop(0, CHUNKS, finish_stats, 0)

    def to_send(at):
        gsend[at, 0] = (dkv[0] * SCALE).astype(BF16)
        gsend[at, 1] = dkv[1].astype(BF16)

    def add(at, weight):
        dkv[0] += grecv[at, 0].astype(F32) * (weight / SCALE)
        dkv[1] += grecv[at, 1].astype(F32) * weight

    weight_row(0)
    backward_a(1)
    to_send(0)
    grad_1 = send(gsend.at[0], grecv.at[0], me.sibling())
    weight_quad(1)
    backward_a(3)
    to_send(1)
    grad_3 = send(gsend.at[1], grecv.at[1], me.sibling())
    weight_quad(3)
    to_row(0)
    backward_a(2)
    grad_1.wait_recv()
    grad_3.wait_recv()
    add(1 - core, 1.0)
    to_send(2)
    grad_2 = send(gsend.at[2], grecv.at[2], me.chip(-1))
    weight_quad(2)
    to_row(1)
    backward_a(4)
    add(1, core.astype(F32))
    to_send(3)
    grad_4 = send(gsend.at[3], grecv.at[3], me.chip(-2))
    weight_row(1)
    backward_a(0)

    def finish_dq(c, _):
        dq_ref[pl.ds(c * CHUNK, CHUNK), :] = (dqt[c] * SCALE).T.astype(BF16)
        return 0

    lax.fori_loop(0, CHUNKS, finish_dq, 0)
    stores = [pltpu.make_async_copy(dq_ref, dq_hbm, load_sem.at[7])]
    stores[0].start()
    add(0, (1 - core).astype(F32))
    to_row(2)
    weight_row(2)
    to_row(3)
    weight_row(3)
    grad_2.wait_recv()
    grad_4.wait_recv()
    add(2, 1.0)
    add(3, 1.0)
    dk_ref[...] = (dkv[0] * SCALE).astype(BF16)
    dv_ref[...] = dkv[1].astype(BF16)
    stores.append(pltpu.make_async_copy(dk_ref, dk_hbm, load_sem.at[8]))
    stores.append(pltpu.make_async_copy(dv_ref, dv_hbm, load_sem.at[9]))
    stores[1].start()
    stores[2].start()

    in_chip = all_of(wt.at[1 - core], 1, 0)
    in_head = all_of(att.at[pl.ds(0, 6)], 4, 3)
    in_chip.wait_recv()
    in_head.wait_recv()
    total = None
    for q in range(4):
        for hi in range(2):
            head = (hi * 4 + q - 1) % Z
            rhs = jnp.concatenate(
                [
                    jnp.concatenate([wt[k, y, q, hi, h] for y in range(Y) for k in range(2)], axis=0)
                    for h in range(HEADS)
                ],
                axis=1,
            )
            lhs = jnp.concatenate(
                [
                    jnp.concatenate([att[head, c, h] for c in range(CHUNKS)], axis=0)
                    for h in range(HEADS)
                ],
                axis=1,
            )
            term = nt(lhs, rhs)
            total = term if total is None else total + term
    out_ref[...] = total.astype(BF16)
    for store in stores:
        store.wait()
    for copy in started:
        copy.wait_send()
    in_chip.wait_send()
    in_head.wait_send()
    all_of(wt.at[0, pl.ds(0, 3)], 2, 0).wait_send()

    @pl.when(even_chip)
    def _():
        for copy in from_even:
            copy.wait_send()

    assert taken == [SENDS, RECVS], taken


SENDS, RECVS = 20, 32


def place(*refs):
    ins, outs, held, sems = refs[:4], refs[4:8], refs[8:12], refs[12]
    loads = [pltpu.make_async_copy(ins[i], held[i], sems.at[i]) for i in range(4)]
    for load in loads:
        load.start()
    stores = []
    for i in range(4):
        loads[i].wait()
        stores.append(pltpu.make_async_copy(held[i], outs[i], sems.at[4 + i]))
        stores[i].start()
    for store in stores:
        store.wait()


def local(block_order, query_b, key_b, value_b, out_weight, query_a, key_a, value_a, grad_a):
    flat_q = lambda a: a.reshape(QROWS, DIM)
    flat_k = lambda a: a.reshape(ROWS, DIM)
    vmem = pl.BlockSpec(memory_space=pltpu.VMEM)
    results = pl.pallas_call(
        kernel,
        out_shape=(
            jax.ShapeDtypeStruct((ROWS, 512), BF16),
            jax.ShapeDtypeStruct((QROWS, DIM), BF16),
            jax.ShapeDtypeStruct((ROWS, DIM), BF16),
            jax.ShapeDtypeStruct((ROWS, DIM), BF16),
        ),
        in_specs=[pl.BlockSpec(memory_space=pltpu.SMEM)] + [pl.BlockSpec(memory_space=pl.ANY)] * 8,
        out_specs=(vmem,) + (pl.BlockSpec(memory_space=pl.ANY),) * 3,
        scratch_shapes=[
            pltpu.VMEM((QROWS, DIM), BF16),
            pltpu.VMEM((ROWS, DIM), BF16),
            pltpu.VMEM((ROWS, DIM), BF16),
            pltpu.VMEM((QROWS, DIM), BF16),
            pltpu.VMEM((QROWS, DIM), BF16),
            pltpu.VMEM((QROWS, DIM), BF16),
            pltpu.VMEM((5, 2, ROWS, DIM), BF16),
            pltpu.VMEM((5, 2, ROWS, DIM), BF16),
            pltpu.VMEM((2, Y, 4, 2, HEADS, 64, DIM), BF16),
            pltpu.VMEM((8, CHUNKS, HEADS, CHUNK // HEADS, DIM), BF16),
            pltpu.VMEM((5, CHUNKS, ROWS, CHUNK), F32),
            pltpu.VMEM((5, CHUNKS, ROWS, CHUNK), F32),
            pltpu.VMEM((CHUNK, DIM), F32),
            pltpu.VMEM((CHUNKS, DIM, CHUNK), F32),
            pltpu.VMEM((CHUNKS, DIM, CHUNK), F32),
            pltpu.VMEM((CHUNKS, 1, CHUNK), F32),
            pltpu.VMEM((CHUNKS, 1, CHUNK), F32),
            pltpu.VMEM((CHUNKS, 1, CHUNK), F32),
            pltpu.VMEM((CHUNKS, 1, CHUNK), F32),
            pltpu.VMEM((CHUNKS, 1, CHUNK), F32),
            pltpu.VMEM((5, DIM, ROWS), BF16),
            pltpu.VMEM((5, CHUNKS, ROWS, CHUNK), F32),
            pltpu.VMEM((2, ROWS, DIM), F32),
            pltpu.VMEM((4, 2, ROWS, DIM), BF16),
            pltpu.VMEM((4, 2, ROWS, DIM), BF16),
            pltpu.SemaphoreType.DMA((SENDS,)),
            pltpu.SemaphoreType.DMA((RECVS,)),
            pltpu.SemaphoreType.DMA((5,)),
            pltpu.SemaphoreType.DMA((10,)),
            pltpu.SemaphoreType.DMA((2,)),
            pltpu.SemaphoreType.DMA((2,)),
        ],
        compiler_params=pltpu.CompilerParams(
            collective_id=0, has_side_effects=True, vmem_limit_bytes=62 * 2**20
        ),
        name="attention",
    )(
        block_order, flat_q(query_b), flat_k(key_b), flat_k(value_b),
        jnp.transpose(out_weight, (0, 2, 1)),
        flat_q(query_a), flat_k(key_a), flat_k(value_a), flat_q(grad_a),
    )
    shapes = tuple(jax.ShapeDtypeStruct(a.shape, a.dtype) for a in results)
    out, dq, dk, dv = pl.pallas_call(
        place,
        out_shape=shapes,
        in_specs=[pl.BlockSpec(memory_space=pl.ANY)] * 4,
        out_specs=(pl.BlockSpec(memory_space=pl.ANY),) * 4,
        scratch_shapes=[pltpu.VMEM(a.shape, a.dtype) for a in results]
        + [pltpu.SemaphoreType.DMA((8,))],
        compiler_params=pltpu.CompilerParams(vmem_limit_bytes=62 * 2**20),
        name="place",
    )(*results)
    flat = (ROWS, 1, DIM)
    return out, dq.reshape(ROWS, HEADS, DIM), dk.reshape(flat), dv.reshape(flat)


def solution(mesh):
    heads = P("ctx", "head", None)
    return jax.shard_map(
        local,
        mesh=mesh,
        in_specs=(P("ctx"), heads, heads, heads, P("head", None, "ctx"), heads, heads, heads, heads),
        out_specs=(P("ctx", "head"), heads, heads, heads),
        check_vma=False,
    )
```
